256 devices in a mesh: tm: 16 (over z, core), tile: 16 (over y, x).
Axes of the slice: x: 4, y: 4, z: 8, core: 2. Of those that a mesh axis runs over, the one named last changes fastest.
Arguments:
- boundary_inv: float32 [16, 1024, 1024], P('tm', 'tile'), may hold values from -1 to 1, as said below
- coupling: bfloat16 [16, 1024, 1024], P('tm', 'tile'), may hold values from -2 to 2
- interior_map: bfloat16 [16, 4, 1024, 1024], P('tm'), may hold values from -0.1875 to 0.1875
- interior_inv: float32 [16, 4, 1024, 1024], P('tm', None, 'tile'), may hold values from -1 to 2, as said below
Outputs:
- boundary_cov: float32 [16, 1024, 1024], P('tm', 'tile')
- interior_cov: float32 [16, 4, 1024, 1024], P('tm', None, 'tile')
The draws below stay inside these ranges and needn't reach their ends.
Inputs may be any that keep to these rules, and one draw needn't show every extreme that they name: `boundary_inv`: each block is symmetric. `interior_inv`: each block is symmetric.
All inputs are finite; a program needn't handle non-finite values.
Results may differ from the reference program's by a relative error of at most 0.0041.
Values may be sent and summed in bfloat16 or wider, within the bound.
No kernel may reach another device: no remote copies, remote signals or barrier semaphores. Data moves between devices by JAX's collectives and lax.ppermute only.
A program may use at most 64 MiB of HBM per device.

```python
import math
import jax
import jax.numpy as jnp
from jax import lax

BLOCK = 1024
INTERIOR = 4
PARTS_SIZE = 16
LEVELS = 4


def symmetric_blocks(key, shape, low, high, spread):
    key_diag, key_noise = jax.random.split(key, 2)
    size = shape[-1]
    diag_values = jnp.exp(jax.random.uniform(key_diag, shape[:-1], jnp.float32, math.log(low), math.log(high)))
    normal_part = jax.random.truncated_normal(key_noise, -4.0, 4.0, shape, jnp.float32)
    noise = normal_part
    paired = (noise + jnp.swapaxes(noise, -1, -2)) * (spread / math.sqrt(2.0 * size))
    return paired + jnp.eye(size, dtype=jnp.float32) * diag_values[..., None]


def draw_boundary_inv(key, part):
    key = jax.random.fold_in(key, 1)
    return symmetric_blocks(key, (PARTS_SIZE, BLOCK, BLOCK), 0.05, 0.15, 0.02)


def draw_interior_inv(key, part):
    key = jax.random.fold_in(key, 3)
    return symmetric_blocks(key, (PARTS_SIZE, INTERIOR, BLOCK, BLOCK), 0.3, 1.0, 0.12)


def signed_table(key_perm, key_rows, key_cols):
    row_order = jax.vmap(lambda one_key: jax.random.permutation(one_key, BLOCK))(jax.random.split(key_perm, PARTS_SIZE)).astype(jnp.int32)
    col_index = jnp.arange(BLOCK, dtype=jnp.int32)
    common = jnp.bitwise_and(row_order[:, :, None], col_index[None, None, :])
    parity = jnp.zeros(common.shape, jnp.int32)
    for position in range(BLOCK.bit_length()):
        parity = parity + jnp.bitwise_and(jnp.right_shift(common, position), 1)
    bit_parity = parity % 2
    sign_table = (1 - 2 * bit_parity).astype(jnp.float32)
    row_signs = (2 * jax.random.randint(key_rows, (PARTS_SIZE, BLOCK, 1), 0, 2) - 1).astype(jnp.float32)
    col_signs = (2 * jax.random.randint(key_cols, (PARTS_SIZE, 1, BLOCK), 0, 2) - 1).astype(jnp.float32)
    return sign_table * row_signs * col_signs


def draw_coupling(key, part):
    key = jax.random.fold_in(key, 2)
    key_perm, key_rows, key_cols, key_noise, key_scale = jax.random.split(key, 5)
    shape = (PARTS_SIZE, BLOCK, BLOCK)
    jitter = jax.random.truncated_normal(key_noise, -4.0, 4.0, shape, jnp.float32)
    strength = 0.95
    scale_low = math.log(0.85)
    col_scales = jnp.exp(jax.random.uniform(key_scale, (PARTS_SIZE, 1, BLOCK), jnp.float32, scale_low, 0.05))
    base = signed_table(key_perm, key_rows, key_cols) + 0.2 * jitter
    return (base * col_scales * (strength / math.sqrt(BLOCK))).astype(jnp.bfloat16)


def block_scale(own_key, extent, cuts, low, high):
    def one(dim, parts):
        heights = jax.random.uniform(jax.random.fold_in(jax.random.fold_in(own_key, 6), dim), (parts,), jnp.float32, low / len(cuts), high / len(cuts))
        return jnp.repeat(jnp.exp(heights), extent[dim] // parts).reshape((-1,) + (1,) * (len(extent) - dim - 1))

    loudness = one(*cuts[0])
    for cut in cuts[1:]:
        loudness = loudness * one(*cut)
    return loudness


def normal_values(stream_key, shape, scale, limit, cuts=(), kind=jnp.bfloat16):
    array = scale * jax.random.normal(stream_key, shape, jnp.float32)
    if cuts:
        array = array * block_scale(stream_key, shape, cuts, -0.22, 0.18)
    return jnp.clip(array, -limit, limit).astype(kind)


def setup_inputs(seed: int = 0) -> dict:
    arg_keys = jax.random.split(jax.random.key(seed), 5)
    boundary_inv = draw_boundary_inv(jax.random.fold_in(arg_keys[4], 71), 0)
    coupling = draw_coupling(jax.random.fold_in(arg_keys[4], 71), 0)
    interior_map = normal_values(arg_keys[2], (PARTS_SIZE, INTERIOR, BLOCK, BLOCK), BLOCK ** -0.5, 0.1875, ((0, 16),))
    interior_inv = draw_interior_inv(jax.random.fold_in(arg_keys[4], 71), 0)
    return {"boundary_inv": boundary_inv, "coupling": coupling, "interior_map": interior_map, "interior_inv": interior_inv}


def reference(boundary_inv, coupling, interior_map, interior_inv):
    sigma_all = boundary_inv
    factor_all = coupling
    for height in range(LEVELS):
        stride = 2 ** height
        keep = PARTS_SIZE - stride
        partner_sigma = sigma_all[stride:].astype(jnp.bfloat16).astype(jnp.float32)
        partner_factor = factor_all[stride:].astype(jnp.float32)
        own_factor = factor_all[:keep].astype(jnp.float32)
        product = jnp.einsum("pab,pbc->pac", partner_sigma, own_factor).astype(jnp.bfloat16)
        update = jnp.einsum("pba,pbc->pac", own_factor, product.astype(jnp.float32))
        sigma_all = jnp.concatenate([sigma_all[:keep] + update, sigma_all[keep:]], 0)
        if height + 1 < LEVELS:
            new_factor = jnp.einsum("pab,pbc->pac", partner_factor, own_factor).astype(jnp.bfloat16)
            factor_all = jnp.concatenate([new_factor, factor_all[keep:]], 0)
    sigma_low = sigma_all.astype(jnp.bfloat16).astype(jnp.float32)

    def one_part(pieces):
        sigma_one, maps_one, local_one = pieces
        maps_wide = maps_one.astype(jnp.float32)
        product = jnp.einsum("ab,jbc->jac", sigma_one, maps_wide).astype(jnp.bfloat16)
        return local_one + jnp.einsum("jba,jbc->jac", maps_wide, product.astype(jnp.float32))

    interior_cov = lax.map(one_part, (sigma_low, interior_map, interior_inv))
    return sigma_all, interior_cov
```

```python
import math

import jax
import jax.numpy as jnp
from jax import lax
from jax.sharding import PartitionSpec as P

AXES = ("tm", "tile")
BF16 = jnp.bfloat16
F32 = jnp.float32


def dot(left, right, left_dim, right_dim):
    return lax.dot_general(
        left, right, (((left_dim,), (right_dim,)), ((), ())), preferred_element_type=F32
    )


def shards(boundary_inv, coupling, interior_map, interior_inv):
    planes = lax.axis_size("tm") // 2
    side = math.isqrt(lax.axis_size("tile"))
    core = lax.axis_index("tm") % 2
    row = lax.axis_index("tile") // side
    col = lax.axis_index("tile") % side
    first = core == 0
    chunk, order = boundary_inv.shape[1:]
    panel = chunk * side

    def move(value, route):
        pairs = []
        for z in range(planes):
            for c in range(2):
                for y in range(side):
                    for x in range(side):
                        to = route(z, c, y, x)
                        if to is not None and 0 <= to[0] < planes:
                            tz, tc, ty, tx = to
                            source = ((2 * z + c) * side + y) * side + x
                            target = ((2 * tz + tc) * side + ty % side) * side + tx % side
                            pairs.append((source, target))
        return lax.ppermute(value, AXES, pairs)

    def swap_cores(value):
        return move(value, lambda z, c, y, x: (z, 1 - c, y, x))

    def from_first(value):
        return move(value, lambda z, c, y, x: (z, 1, y, x) if c == 0 else None)

    def from_second(value):
        return move(value, lambda z, c, y, x: (z, 0, y, x) if c == 1 else None)

    def across(value):
        return [move(value, lambda z, c, y, x: (z, c, x + t, y)) for t in range(side)]

    def spread(value):
        return [
            move(
                value,
                lambda z, c, y, x: (z, c, x + t, y)
                if c == 0
                else ((z, c, y, x + t) if t else None),
            )
            for t in range(side)
        ]

    def from_later(value, stride):
        return [
            move(value, lambda z, c, y, x: (z - stride, c, y + t, x)) for t in range(side)
        ]

    def along_row(pick):
        return [pick(col)] + [
            move(pick((col + t) % side), lambda z, c, y, x: (z, c, y, x + t))
            for t in range(1, side)
        ]

    def by_rows(pieces, place):
        out = jnp.zeros((order, pieces[0].shape[1]), pieces[0].dtype)
        for t, piece in enumerate(pieces):
            start = place(t) % side * piece.shape[0]
            out = lax.dynamic_update_slice_in_dim(out, piece, start, 0)
        return out

    def by_cols(pieces, place):
        out = jnp.zeros((*pieces[0].shape[:-1], order), pieces[0].dtype)
        for t, piece in enumerate(pieces):
            start = place(t) % side * piece.shape[-1]
            out = lax.dynamic_update_slice_in_dim(out, piece, start, out.ndim - 1)
        return out

    b_rows = boundary_inv[0]
    f_rows = coupling[0]
    maps = interior_map[0]
    count = maps.shape[0]

    b_low = b_rows.astype(BF16)
    whole = lax.all_gather(jnp.stack([f_rows, b_low]), "tile", axis=0)
    whole_f = whole[:, 0].reshape(order, order)
    whole_b = whole[:, 1].reshape(order, order)

    blocks = f_rows.reshape(chunk, side, panel).swapaxes(0, 1)
    blocks = jnp.broadcast_to(blocks[:, None], (side, side, chunk, panel))
    blocks = blocks.reshape(side * side, chunk, panel)
    f_panel = lax.all_to_all(blocks, "tile", 0, 0).reshape(side, panel, panel)
    f_panel = f_panel[(row - jnp.arange(side)) % side].reshape(order, panel)
    other = from_first(f_panel)
    f_panel = jnp.where(first, f_panel, other)

    b_odd = from_second(b_low)
    moved = across(jnp.where(first, b_odd, f_rows))
    x_panel = jnp.zeros((panel, order), BF16)
    for t, piece in enumerate(moved):
        x_panel = lax.dynamic_update_slice_in_dim(
            x_panel, piece, (row - t) % side * chunk, 0
        )
    x_panel = x_panel.reshape(panel, side, panel)[:, (row - jnp.arange(side)) % side]
    x_panel = x_panel.reshape(panel, order)

    def b_part(i):
        return lax.dynamic_slice_in_dim(b_rows, i * panel, panel, 1)

    b_block = jnp.zeros((panel, panel), F32)
    for t, piece in enumerate(along_row(b_part)):
        b_block = lax.dynamic_update_slice_in_dim(
            b_block, piece, (col - t) % side * chunk, 0
        )
    sigma = b_block.T

    stride = 1
    levels = planes.bit_length() - 1
    for level in range(levels + 1):
        if level:
            block = jnp.where(first, sigma.astype(BF16), factor)
            x_panel = jnp.concatenate(from_later(block, stride), 1)
            stride *= 2
        product = dot(x_panel, f_panel, 1, 0).astype(BF16)
        factor = product
        moved = spread(product)
        moved[0] = jnp.where(first, moved[0], product)
        w_panel = jnp.concatenate(moved, 0)
        sigma = sigma + dot(w_panel, f_panel, 0, 0)
        if level < levels:
            f_new = by_rows(moved, lambda t: row - col + t)
            other = from_second(f_new)
            f_panel = jnp.where(first, other, f_new)

    low = sigma.astype(BF16)
    other = from_first(low)
    low = jnp.where(first, low, other)
    moved = [
        move(low, lambda z, c, y, x: (z - c, c, y + t, x) if c or t else None)
        for t in range(side)
    ]
    moved[0] = jnp.where(first, low, moved[0])
    s_panel = by_cols(moved, lambda t: row - t)

    eye = jnp.eye(order, dtype=BF16)
    left = jnp.where(first, eye, whole_f)
    h_maps = [dot(left, maps[j], 1, 0).astype(BF16) for j in range(count)]
    own_maps = lax.dynamic_slice_in_dim(
        maps, (row * side + col) * chunk, chunk, 2
    )
    base_rows = jnp.einsum(
        "jbr,bc->jrc", own_maps, jnp.where(first, 0, whole_b), preferred_element_type=F32
    ).astype(BF16)
    base = interior_inv[0] + jnp.einsum(
        "jrb,jbc->jrc", base_rows, maps, preferred_element_type=F32
    )

    lefts = [
        lax.dynamic_slice_in_dim(m, row * panel, panel, 1) for m in h_maps + [whole_f]
    ]
    y_cols = jnp.stack([dot(m, s_panel, 0, 1).astype(BF16) for m in lefts])

    def y_part(i):
        return lax.dynamic_slice_in_dim(y_cols, i * chunk, chunk, 1)

    y_rows = by_cols(along_row(y_part), lambda t: col - t)
    interior_cov = jnp.stack(
        [base[j] + dot(y_rows[j], h_maps[j], 1, 0) for j in range(count)]
    )

    sigma_t = sigma.T

    def s_part(i):
        return lax.dynamic_slice_in_dim(sigma_t, i * chunk, chunk, 0)

    even_rows = by_cols(along_row(s_part), lambda t: col - t)
    odd_rows = b_rows + dot(y_rows[count], whole_f, 1, 0)
    boundary_cov = jnp.where(first, even_rows, odd_rows)
    return boundary_cov[None], interior_cov[None]


def solution(mesh):
    in_specs = (
        P("tm", "tile", None),
        P("tm", "tile", None),
        P("tm", None, None, None),
        P("tm", None, "tile", None),
    )
    out_specs = (P("tm", "tile", None), P("tm", None, "tile", None))
    return jax.shard_map(shards, mesh=mesh, in_specs=in_specs, out_specs=out_specs, check_vma=False)
```

```python
import jax
import jax.numpy as jnp
from jax import lax
from jax.experimental import pallas as pl
from jax.experimental.pallas import tpu as pltpu
from jax.sharding import PartitionSpec as P

AXES = ("tm", "tile")
BF16 = jnp.bfloat16
F32 = jnp.float32


def dot(left, right, left_dim, right_dim):
    return lax.dot_general(
        left, right, (((left_dim,), (right_dim,)), ((), ())), preferred_element_type=F32
    )


def interior_rows(sigma_ref, maps_ref, out_ref):
    sigma = sigma_ref[...]
    one, two = [
        jnp.dot(sigma, maps_ref[j], preferred_element_type=F32) for j in range(2)
    ]
    rows, width = out_ref.shape[1:]
    low = lax.broadcasted_iota(jnp.int32, (rows, width), 1) < width // 2
    for pair in range(out_ref.shape[0] // 2):
        a = one[:, pair * width : (pair + 1) * width]
        b = two[:, pair * width : (pair + 1) * width]
        even = jnp.where(low, a, pltpu.roll(b, width // 2, 1))
        odd = jnp.where(low, pltpu.roll(a, width // 2, 1), b)
        out_ref[2 * pair] = even.astype(BF16)
        out_ref[2 * pair + 1] = odd.astype(BF16)


def interior_sums(cols_ref, maps_ref, inv_ref, out_ref):
    rows = inv_ref.shape[1]
    turned = cols_ref[...].T
    for j in range(2):
        out_ref[j] = inv_ref[j] + jnp.dot(
            turned[j * rows : (j + 1) * rows], maps_ref[j], preferred_element_type=F32
        )


def shards(boundary_inv, coupling, interior_map, interior_inv):
    planes = lax.axis_size("tm") // 2
    tiles = lax.axis_size("tile")
    first = lax.axis_index("tm") % 2 == 0
    chunk, order = boundary_inv.shape[1:]
    half = order // 2

    def move(value, route):
        pairs = []
        for z in range(planes):
            for c in range(2):
                to = route(z, c)
                if to is not None and 0 <= to[0] < planes:
                    for t in range(tiles):
                        source, target = 2 * z + c, 2 * to[0] + to[1]
                        pairs.append((source * tiles + t, target * tiles + t))
        return lax.ppermute(value, AXES, pairs)

    def swap_cores(value):
        return move(value, lambda z, c: (z, 1 - c))

    def exchange(pieces):
        return lax.all_to_all(pieces, "tile", 0, 0)

    def gather(value):
        return exchange(jnp.broadcast_to(value, (tiles, *value.shape)))

    def times(left, left_dim, halves):
        mine, other = [dot(left, h, left_dim, 0) for h in halves]
        return jnp.concatenate(
            [jnp.where(first, mine, other), jnp.where(first, other, mine)], 1
        )

    def cut(value):
        pieces = value.reshape(chunk, tiles, chunk).swapaxes(0, 1)
        return jnp.concatenate([pieces, jnp.zeros_like(pieces)], 2)

    def turn(value):
        return exchange(cut(value)).reshape(order, 2 * chunk)[:, :chunk]

    b_rows = boundary_inv[0]
    f_rows = coupling[0]
    maps = interior_map[0]
    count = maps.shape[0]

    give = jnp.where(first, f_rows[:, half:], f_rows[:, :half])
    given = swap_cores(jnp.concatenate([b_rows.astype(BF16), give], 1))
    x_rows = jnp.where(first, given[:, :order], f_rows)
    even_half = jnp.where(first, f_rows[:, :half], given[:, order:])
    odd_half = jnp.where(first, given[:, order:], f_rows[:, half:])

    odd_mine = lax.all_gather(odd_half, "tile", axis=0, tiled=True)

    f_mine = gather(even_half).reshape(order, half)
    sigma = b_rows
    levels = planes.bit_length() - 1
    for level in range(levels + 1):
        last = level == levels
        if level:
            hop = 2 ** (level - 1)
            block = jnp.where(first, sigma.astype(BF16), product)
            x_rows = move(block, lambda z, c: None if last and c else (z - hop, c))
        halves = (f_mine, swap_cores(f_mine))
        product = times(x_rows, 1, halves).astype(BF16)
        if last:
            w_cols = turn(product)
        else:
            new_half = move(
                product[:, :half], lambda z, c: (z, 0) if c else None
            )
            new_half = jnp.where(first, new_half, product[:, half:])
            pieces = jnp.concatenate(
                [
                    jnp.broadcast_to(new_half, (tiles, chunk, half)),
                    cut(product),
                ],
                2,
            )
            pieces = exchange(pieces).reshape(order, half + 2 * chunk)
            w_cols = pieces[:, half : half + chunk]
            f_mine = pieces[:, :half]
        sigma = sigma + times(w_cols, 0, halves)

    low = sigma.astype(BF16)
    x_rows = move(low, lambda z, c: (z - 1, 1) if c == 0 else None)
    odd_other = move(odd_mine, lambda z, c: (z, 1) if c == 0 else None)
    halves = (odd_mine, odd_other)
    w_cols = turn(times(x_rows, 1, halves).astype(BF16))
    sigma = jnp.where(first, sigma, b_rows + times(w_cols, 0, halves))

    low = sigma.astype(BF16)
    params = pltpu.CompilerParams(vmem_limit_bytes=40 * 2**20)
    cost = pl.CostEstimate(
        flops=2 * count * chunk * order * order,
        bytes_accessed=2 * count * order * order,
        transcendentals=0,
    )
    v_rows = pl.pallas_call(
        interior_rows,
        grid=(count // 2,),
        in_specs=[
            pl.BlockSpec((chunk, order), lambda j: (0, 0)),
            pl.BlockSpec((2, order, order), lambda j: (j, 0, 0)),
        ],
        out_specs=pl.BlockSpec((tiles, chunk, 2 * chunk), lambda j: (0, 0, j)),
        out_shape=jax.ShapeDtypeStruct((tiles, chunk, count * chunk), BF16),
        compiler_params=params,
        cost_estimate=cost,
    )(low, maps)
    v_cols = exchange(v_rows).reshape(order, count * chunk)
    interior_cov = pl.pallas_call(
        interior_sums,
        grid=(count // 2,),
        in_specs=[
            pl.BlockSpec((order, 2 * chunk), lambda j: (0, j)),
            pl.BlockSpec((2, order, order), lambda j: (j, 0, 0)),
            pl.BlockSpec((2, chunk, order), lambda j: (j, 0, 0)),
        ],
        out_specs=pl.BlockSpec((2, chunk, order), lambda j: (j, 0, 0)),
        out_shape=jax.ShapeDtypeStruct((count, chunk, order), F32),
        compiler_params=params,
        cost_estimate=cost,
    )(v_cols, maps, interior_inv[0])
    return sigma[None], interior_cov[None]


def solution(mesh):
    in_specs = (
        P("tm", "tile", None),
        P("tm", "tile", None),
        P("tm", None, None, None),
        P("tm", None, "tile", None),
    )
    out_specs = (P("tm", "tile", None), P("tm", None, "tile", None))
    return jax.shard_map(shards, mesh=mesh, in_specs=in_specs, out_specs=out_specs, check_vma=False)
```

```python
import jax
import jax.numpy as jnp
from jax import lax
from jax.experimental import pallas as pl
from jax.experimental.pallas import tpu as pltpu
from jax.sharding import PartitionSpec as P

AXES = ("tm", "tile")
BF16 = jnp.bfloat16
F32 = jnp.float32


def dot(left, right, left_dim, right_dim):
    return lax.dot_general(
        left, right, (((left_dim,), (right_dim,)), ((), ())), preferred_element_type=F32
    )


def interior_rows(sigma_ref, maps_ref, out_ref):
    sigma = sigma_ref[...]
    count = maps_ref.shape[0]
    here, rows, width = out_ref.shape
    lane = 2 * width // count
    low = lax.broadcasted_iota(jnp.int32, (rows, lane), 1) < lane // 2
    for j in range(0, count, 2):
        one, two = [
            jnp.dot(sigma, maps_ref[j + i], preferred_element_type=F32) for i in range(2)
        ]
        to = pl.ds(j // 2 * lane, lane)
        for pair in range(here // 2):
            a = one[:, pair * lane : (pair + 1) * lane]
            b = two[:, pair * lane : (pair + 1) * lane]
            even = jnp.where(low, a, pltpu.roll(b, lane // 2, 1))
            odd = jnp.where(low, pltpu.roll(a, lane // 2, 1), b)
            out_ref[2 * pair, :, to] = even.astype(BF16)
            out_ref[2 * pair + 1, :, to] = odd.astype(BF16)


def interior_sums(cols_ref, maps_ref, inv_ref, out_ref):
    count, rows = inv_ref.shape[:2]
    turned = cols_ref[...].T
    for j in range(count):
        out_ref[j] = inv_ref[j] + jnp.dot(
            turned[j * rows : (j + 1) * rows], maps_ref[j], preferred_element_type=F32
        )


def shards(boundary_inv, coupling, interior_map, interior_inv):
    planes = lax.axis_size("tm") // 2
    tiles = lax.axis_size("tile")
    first = lax.axis_index("tm") % 2 == 0
    chunk, order = boundary_inv.shape[1:]
    half = order // 2

    def move(value, route):
        pairs = []
        for z in range(planes):
            for c in range(2):
                to = route(z, c)
                if to is not None and 0 <= to[0] < planes:
                    for t in range(tiles):
                        source, target = 2 * z + c, 2 * to[0] + to[1]
                        pairs.append((source * tiles + t, target * tiles + t))
        return lax.ppermute(value, AXES, pairs)

    def swap_cores(value):
        return move(value, lambda z, c: (z, 1 - c))

    def from_first(value):
        return move(value, lambda z, c: (z, 1) if c == 0 else None)

    def from_second(value):
        return move(value, lambda z, c: (z, 0) if c else None)

    def exchange(pieces):
        return lax.all_to_all(pieces, "tile", 0, 0)

    def gather(value):
        return exchange(jnp.broadcast_to(value, (tiles, *value.shape)))

    def cut(value):
        pairs = value.reshape(chunk, tiles // 2, 2 * chunk).swapaxes(0, 1)
        turned = jnp.roll(pairs, chunk, 2)
        return jnp.stack([pairs, turned], 1).reshape(tiles, chunk, 2 * chunk)

    def times(left, left_dim, halves):
        return jnp.concatenate([dot(left, h, left_dim, 0) for h in halves], 1)

    def fold(w_cols, halves):
        return times(w_cols, 0, halves)[:chunk]

    def turn(value):
        return exchange(cut(value)).reshape(order, 2 * chunk)

    b_rows = boundary_inv[0]
    f_rows = coupling[0]
    maps = interior_map[0]
    count = maps.shape[0]

    given = swap_cores(jnp.concatenate([f_rows, b_rows.astype(BF16)], 1))
    s_rows = given[:, order:]
    q_rows = jnp.where(first, given[:, :order], f_rows)
    f_half = jnp.where(first, f_rows[:, :half], given[:, half:order])
    odd = jnp.where(first, given[:, :half], f_rows[:, half:])

    pieces = gather(jnp.concatenate([f_half, odd], 1)).reshape(order, order)
    f_mine, odd = pieces[:, :half], pieces[:, half:]
    f_halves = (f_mine, from_second(f_mine))
    odd_other = swap_cores(odd)

    w_rows = times(s_rows, 1, f_halves).astype(BF16)
    own = jnp.where(first, 0, half)
    f_mine = (
        dot(odd, lax.dynamic_slice_in_dim(f_mine, own, half, 0), 1, 0)
        + dot(odd_other, lax.dynamic_slice_in_dim(f_mine, half - own, half, 0), 1, 0)
    ).astype(BF16)
    q_half = lax.dynamic_slice_in_dim(f_mine, lax.axis_index("tile") * chunk, chunk, 0)
    q_half = move(q_half, lambda z, c: (z - 1, c))
    other = swap_cores(q_half)
    sigma = b_rows + fold(turn(w_rows), f_halves)

    f_halves = (f_mine, from_second(f_mine))
    s_rows = move(sigma.astype(BF16), lambda z, c: None if c else (z - 1, c))
    q_rows = jnp.concatenate(
        [jnp.where(first, q_half, other), jnp.where(first, other, q_half)], 1
    )
    f_half = dot(q_rows, f_mine, 1, 0).astype(BF16)
    w_rows = times(s_rows, 1, f_halves).astype(BF16)
    pieces = jnp.concatenate(
        [jnp.broadcast_to(f_half, (tiles, chunk, half)), cut(w_rows)], 2
    )
    pieces = exchange(pieces).reshape(order, half + 2 * chunk)
    sigma = sigma + fold(pieces[:, half:], f_halves)

    f_mine = pieces[:, :half]
    f_halves = (f_mine, from_second(f_mine))
    for done in range(planes - 2, 0, -2):
        s_rows = move(
            sigma.astype(BF16),
            lambda z, c: (z - 2, c) if c == 0 and z in (done, done + 1) else None,
        )
        w_rows = times(s_rows, 1, f_halves).astype(BF16)
        sigma = sigma + fold(turn(w_rows), f_halves)

    x_rows = move(
        sigma.astype(BF16), lambda z, c: (z - 1, 1) if c == 0 else None
    )
    odd_halves = (odd_other, odd)
    w_rows = times(x_rows, 1, odd_halves).astype(BF16)
    update = fold(turn(w_rows), odd_halves)
    sigma = jnp.where(first, sigma, b_rows + update)

    low = sigma.astype(BF16)
    params = pltpu.CompilerParams(vmem_limit_bytes=40 * 2**20)
    cost = pl.CostEstimate(
        flops=2 * count * chunk * order * order,
        bytes_accessed=2 * count * order * order,
        transcendentals=0,
    )
    two = count // 2
    map_spec = pl.BlockSpec((two, order, order), lambda n: (n, 0, 0))
    sum_spec = pl.BlockSpec((two, chunk, order), lambda n: (n, 0, 0))
    v_rows = pl.pallas_call(
        interior_rows,
        grid=(2,),
        in_specs=[pl.BlockSpec((chunk, order), lambda n: (0, 0)), map_spec],
        out_specs=pl.BlockSpec((tiles, chunk, two * chunk), lambda n: (0, 0, n)),
        out_shape=jax.ShapeDtypeStruct((tiles, chunk, count * chunk), BF16),
        compiler_params=params,
        cost_estimate=cost,
    )(low, maps)
    v_cols = exchange(v_rows).reshape(order, count * chunk)
    interior_cov = pl.pallas_call(
        interior_sums,
        grid=(2,),
        in_specs=[
            pl.BlockSpec((order, two * chunk), lambda n: (0, n)),
            map_spec,
            sum_spec,
        ],
        out_specs=sum_spec,
        out_shape=jax.ShapeDtypeStruct((count, chunk, order), F32),
        compiler_params=params,
        cost_estimate=cost,
    )(v_cols, maps, interior_inv[0])
    return sigma[None], interior_cov[None]


def solution(mesh):
    in_specs = (
        P("tm", "tile", None),
        P("tm", "tile", None),
        P("tm", None, None, None),
        P("tm", None, "tile", None),
    )
    out_specs = (P("tm", "tile", None), P("tm", None, "tile", None))
    return jax.shard_map(shards, mesh=mesh, in_specs=in_specs, out_specs=out_specs, check_vma=False)
```

```python
import functools

import jax
import jax.numpy as jnp
from jax import lax
from jax.experimental import pallas as pl
from jax.experimental.pallas import tpu as pltpu
from jax.sharding import PartitionSpec as P

AXES = ("tm", "tile")
BF16 = jnp.bfloat16
F32 = jnp.float32


def dot(left, right, left_dim, right_dim):
    return lax.dot_general(
        left, right, (((left_dim,), (right_dim,)), ((), ())), preferred_element_type=F32
    )


def spread_rows(rows_ref, out_ref):
    for t in range(out_ref.shape[0]):
        out_ref[t] = rows_ref[...]


def spread_products(with_rows, s_ref, rows_ref, mine_ref, other_ref, out_ref):
    tiles, rows, width = out_ref.shape
    lane = 2 * rows
    start = width - lane
    if with_rows is not None:
        all_rows = rows_ref[...]
        if with_rows:
            all_rows = jnp.dot(all_rows, mine_ref[...], preferred_element_type=F32)
            all_rows = all_rows.astype(BF16)
        for t in range(tiles):
            out_ref[t, :, :start] = all_rows
    t = 0
    for ref in (mine_ref, other_ref):
        product = jnp.dot(s_ref[...], ref[...], preferred_element_type=F32)
        for at in range(0, product.shape[1], lane):
            pair = product[:, at : at + lane]
            out_ref[t, :, start:] = pair.astype(BF16)
            out_ref[t + 1, :, start:] = pltpu.roll(pair, rows, 1).astype(BF16)
            t += 2


def interior_rows(sigma_ref, maps_ref, out_ref):
    sigma = sigma_ref[...]
    count = maps_ref.shape[0]
    here, rows, width = out_ref.shape
    lane = 2 * width // count
    low = lax.broadcasted_iota(jnp.int32, (rows, lane), 1) < lane // 2
    for j in range(0, count, 2):
        one, two = [
            jnp.dot(sigma, maps_ref[j + i], preferred_element_type=F32) for i in range(2)
        ]
        to = pl.ds(j // 2 * lane, lane)
        for pair in range(here // 2):
            a = one[:, pair * lane : (pair + 1) * lane]
            b = two[:, pair * lane : (pair + 1) * lane]
            even = jnp.where(low, a, pltpu.roll(b, lane // 2, 1))
            odd = jnp.where(low, pltpu.roll(a, lane // 2, 1), b)
            out_ref[2 * pair, :, to] = even.astype(BF16)
            out_ref[2 * pair + 1, :, to] = odd.astype(BF16)


def interior_sums(cols_ref, maps_ref, inv_ref, out_ref):
    count, rows = inv_ref.shape[:2]
    turned = cols_ref[...].T
    for j in range(count):
        out_ref[j] = inv_ref[j] + jnp.dot(
            turned[j * rows : (j + 1) * rows], maps_ref[j], preferred_element_type=F32
        )


def shards(boundary_inv, coupling, interior_map, interior_inv):
    planes = lax.axis_size("tm") // 2
    tiles = lax.axis_size("tile")
    first = lax.axis_index("tm") % 2 == 0
    chunk, order = boundary_inv.shape[1:]
    half = order // 2

    def move(value, route):
        pairs = []
        for z in range(planes):
            for c in range(2):
                to = route(z, c)
                if to is not None and 0 <= to[0] < planes:
                    for t in range(tiles):
                        source, target = 2 * z + c, 2 * to[0] + to[1]
                        pairs.append((source * tiles + t, target * tiles + t))
        return lax.ppermute(value, AXES, pairs)

    def swap_cores(value):
        return move(value, lambda z, c: (z, 1 - c))

    def from_first(value):
        return move(value, lambda z, c: (z, 1) if c == 0 else None)

    def from_second(value):
        return move(value, lambda z, c: (z, 0) if c else None)

    def exchange(pieces):
        return lax.all_to_all(pieces, "tile", 0, 0)

    def gather(value):
        return exchange(placed(spread_rows, value.shape[1])(value))

    def placed(kernel, width):
        return pl.pallas_call(
            kernel,
            out_shape=pltpu.VMEM((tiles, chunk, width), BF16),
            compiler_params=pltpu.CompilerParams(vmem_limit_bytes=12 * 2**20),
        )

    def times(left, left_dim, halves):
        return jnp.concatenate([dot(left, h, left_dim, 0) for h in halves], 1)

    def fold(w_cols, halves):
        return times(w_cols, 0, halves)[:chunk]

    def turn(s_rows, f_halves):
        pieces = placed(functools.partial(spread_products, None), 2 * chunk)(
            s_rows, s_rows, *f_halves
        )
        return exchange(pieces).reshape(order, 2 * chunk)

    def share(with_rows, s_rows, rows, f_halves):
        pieces = placed(functools.partial(spread_products, with_rows), half + 2 * chunk)(
            s_rows, rows, *f_halves
        )
        return pieces

    b_rows = boundary_inv[0]
    f_rows = coupling[0]
    maps = interior_map[0]
    count = maps.shape[0]

    given = swap_cores(jnp.concatenate([f_rows, b_rows.astype(BF16)], 1))
    s_rows = given[:, order:]
    q_rows = jnp.where(first, given[:, :order], f_rows)
    f_half = jnp.where(first, f_rows[:, :half], given[:, half:order])
    odd = jnp.where(first, given[:, :half], f_rows[:, half:])

    def after(value, anchor):
        return lax.optimization_barrier((value, anchor))[0]

    f_mine = gather(f_half).reshape(order, half)
    f_halves = (f_mine, from_second(f_mine))

    q_half = dot(q_rows, f_mine, 1, 0).astype(BF16)
    q_half = move(q_half, lambda z, c: (z - 1, c))
    pieces = share(False, s_rows, odd, f_halves)
    pieces, q_half = lax.optimization_barrier((pieces, q_half))
    other = swap_cores(q_half)
    pieces = exchange(pieces).reshape(order, half + 2 * chunk)
    odd = pieces[:, :half]
    odd_other = swap_cores(odd)
    sigma = b_rows + fold(pieces[:, half:], f_halves)
    low = sigma.astype(BF16)

    own = jnp.where(first, 0, half)
    f_halves = [
        dot(odd, lax.dynamic_slice_in_dim(f, own, half, 0), 1, 0)
        + dot(odd_other, lax.dynamic_slice_in_dim(f, half - own, half, 0), 1, 0)
        for f in after(f_halves, low)
    ]
    f_halves = [f.astype(BF16) for f in f_halves]
    s_rows = move(low, lambda z, c: None if c else (z - 1, c))
    q_rows = jnp.concatenate(
        [jnp.where(first, q_half, other), jnp.where(first, other, q_half)], 1
    )
    pieces = share(True, s_rows, q_rows, f_halves)
    pieces = exchange(pieces).reshape(order, half + 2 * chunk)
    sigma = sigma + fold(pieces[:, half:], f_halves)
    low = sigma.astype(BF16)
    f_mine = after(pieces[:, :half], low)
    f_halves = (f_mine, from_second(f_mine))

    for done in range(planes - 2, 0, -2):
        s_rows = move(
            low,
            lambda z, c: (z - 2, c) if c == 0 and z in (done, done + 1) else None,
        )
        sigma = sigma + fold(turn(s_rows, f_halves), f_halves)
        low = sigma.astype(BF16)

    x_rows = move(low, lambda z, c: (z - 1, 1) if c == 0 else None)
    odd_halves = (odd_other, odd)
    update = fold(turn(x_rows, odd_halves), odd_halves)
    sigma = jnp.where(first, sigma, b_rows + update)

    low = sigma.astype(BF16)
    params = pltpu.CompilerParams(vmem_limit_bytes=20 * 2**20)
    cost = pl.CostEstimate(
        flops=2 * count * chunk * order * order,
        bytes_accessed=2 * count * order * order,
        transcendentals=0,
    )
    two = count // 2
    map_spec = pl.BlockSpec((two, order, order), lambda n: (n, 0, 0))
    sum_spec = pl.BlockSpec((two, chunk, order), lambda n: (n, 0, 0))
    v_rows = pl.pallas_call(
        interior_rows,
        grid=(2,),
        in_specs=[pl.BlockSpec((chunk, order), lambda n: (0, 0)), map_spec],
        out_specs=pl.BlockSpec((tiles, chunk, two * chunk), lambda n: (0, 0, n)),
        out_shape=jax.ShapeDtypeStruct((tiles, chunk, count * chunk), BF16),
        compiler_params=params,
        cost_estimate=cost,
    )(low, maps)
    v_cols = exchange(v_rows).reshape(order, count * chunk)
    interior_cov = pl.pallas_call(
        interior_sums,
        grid=(2,),
        in_specs=[
            pl.BlockSpec((order, two * chunk), lambda n: (0, n)),
            map_spec,
            sum_spec,
        ],
        out_specs=sum_spec,
        out_shape=jax.ShapeDtypeStruct((count, chunk, order), F32),
        compiler_params=params,
        cost_estimate=cost,
    )(v_cols, maps, interior_inv[0])
    return sigma[None], interior_cov[None]


def solution(mesh):
    in_specs = (
        P("tm", "tile", None),
        P("tm", "tile", None),
        P("tm", None, None, None),
        P("tm", None, "tile", None),
    )
    out_specs = (P("tm", "tile", None), P("tm", None, "tile", None))
    return jax.shard_map(shards, mesh=mesh, in_specs=in_specs, out_specs=out_specs, check_vma=False)
```

```python
import functools

import jax
import jax.numpy as jnp
from jax import lax
from jax.experimental import pallas as pl
from jax.experimental.pallas import tpu as pltpu
from jax.sharding import PartitionSpec as P

AXES = ("tm", "tile")
BF16 = jnp.bfloat16
F32 = jnp.float32


def dot(left, right, left_dim, right_dim):
    return lax.dot_general(
        left, right, (((left_dim,), (right_dim,)), ((), ())), preferred_element_type=F32
    )


def spread_rows(rows_ref, out_ref):
    for t in range(out_ref.shape[0]):
        out_ref[t] = rows_ref[...]


def spread_products(with_rows, s_ref, rows_ref, mine_ref, other_ref, out_ref):
    tiles, rows, width = out_ref.shape
    lane = 2 * rows
    start = width - lane
    if with_rows is not None:
        all_rows = rows_ref[...]
        if with_rows:
            all_rows = jnp.dot(all_rows, mine_ref[...], preferred_element_type=F32)
            all_rows = all_rows.astype(BF16)
        for t in range(tiles):
            out_ref[t, :, :start] = all_rows
    t = 0
    for ref in (mine_ref, other_ref):
        product = jnp.dot(s_ref[...], ref[...], preferred_element_type=F32)
        for at in range(0, product.shape[1], lane):
            pair = product[:, at : at + lane]
            out_ref[t, :, start:] = pair.astype(BF16)
            out_ref[t + 1, :, start:] = pltpu.roll(pair, rows, 1).astype(BF16)
            t += 2


def interior_rows(sigma_ref, maps_ref, out_ref):
    sigma = sigma_ref[...]
    count = maps_ref.shape[0]
    here, rows, width = out_ref.shape
    lane = 2 * width // count
    low = lax.broadcasted_iota(jnp.int32, (rows, lane), 1) < lane // 2
    for j in range(0, count, 2):
        one, two = [
            jnp.dot(sigma, maps_ref[j + i], preferred_element_type=F32) for i in range(2)
        ]
        to = pl.ds(j // 2 * lane, lane)
        for pair in range(here // 2):
            a = one[:, pair * lane : (pair + 1) * lane]
            b = two[:, pair * lane : (pair + 1) * lane]
            even = jnp.where(low, a, pltpu.roll(b, lane // 2, 1))
            odd = jnp.where(low, pltpu.roll(a, lane // 2, 1), b)
            out_ref[2 * pair, :, to] = even.astype(BF16)
            out_ref[2 * pair + 1, :, to] = odd.astype(BF16)


def interior_sums(cols_ref, maps_ref, inv_ref, out_ref):
    count, rows = inv_ref.shape[:2]
    turned = cols_ref[...].T
    for j in range(count):
        out_ref[j] = inv_ref[j] + jnp.dot(
            turned[j * rows : (j + 1) * rows], maps_ref[j], preferred_element_type=F32
        )


def shards(boundary_inv, coupling, interior_map, interior_inv):
    planes = lax.axis_size("tm") // 2
    tiles = lax.axis_size("tile")
    first = lax.axis_index("tm") % 2 == 0
    chunk, order = boundary_inv.shape[1:]
    half = order // 2

    def move(value, route):
        pairs = []
        for z in range(planes):
            for c in range(2):
                to = route(z, c)
                if to is not None and 0 <= to[0] < planes:
                    for t in range(tiles):
                        source, target = 2 * z + c, 2 * to[0] + to[1]
                        pairs.append((source * tiles + t, target * tiles + t))
        return lax.ppermute(value, AXES, pairs)

    def swap_cores(value):
        return move(value, lambda z, c: (z, 1 - c))

    def from_first(value):
        return move(value, lambda z, c: (z, 1) if c == 0 else None)

    def from_second(value):
        return move(value, lambda z, c: (z, 0) if c else None)

    def exchange(pieces):
        return lax.all_to_all(pieces, "tile", 0, 0)

    def gather(value):
        return exchange(placed(spread_rows, value.shape[1])(value))

    def placed(kernel, width):
        return pl.pallas_call(
            kernel,
            out_shape=pltpu.VMEM((tiles, chunk, width), BF16),
            compiler_params=pltpu.CompilerParams(vmem_limit_bytes=12 * 2**20),
        )

    def times(left, left_dim, halves):
        return jnp.concatenate([dot(left, h, left_dim, 0) for h in halves], 1)

    def fold(w_cols, halves):
        return times(w_cols, 0, halves)[:chunk]

    def turn(s_rows, f_halves):
        pieces = placed(functools.partial(spread_products, None), 2 * chunk)(
            s_rows, s_rows, *f_halves
        )
        return exchange(pieces).reshape(order, 2 * chunk)

    def share(with_rows, s_rows, rows, f_halves):
        pieces = placed(functools.partial(spread_products, with_rows), half + 2 * chunk)(
            s_rows, rows, *f_halves
        )
        return pieces

    b_rows = boundary_inv[0]
    f_rows = coupling[0]
    maps = interior_map[0]
    count = maps.shape[0]

    given = swap_cores(f_rows)
    q_rows = jnp.where(first, given, f_rows)
    f_half = jnp.where(first, f_rows[:, :half], given[:, half:])
    odd = jnp.where(first, given[:, :half], f_rows[:, half:])
    s_rows = from_second(b_rows.astype(BF16))

    def after(value, anchor):
        return lax.optimization_barrier((value, anchor))[0]

    f_mine = gather(f_half).reshape(order, half)
    f_halves = (f_mine, from_second(f_mine))

    q_half = dot(q_rows, f_mine, 1, 0).astype(BF16)
    q_half = move(q_half, lambda z, c: (z - 1, c))
    pieces = share(False, s_rows, odd, f_halves)
    other = swap_cores(q_half)
    pieces = exchange(pieces).reshape(order, half + 2 * chunk)
    odd = pieces[:, :half]
    odd_other = swap_cores(odd)
    sigma = b_rows + fold(pieces[:, half:], f_halves)
    low = sigma.astype(BF16)

    own = jnp.where(first, 0, half)
    f_halves = [
        dot(odd, lax.dynamic_slice_in_dim(f, own, half, 0), 1, 0)
        + dot(odd_other, lax.dynamic_slice_in_dim(f, half - own, half, 0), 1, 0)
        for f in after(f_halves, low)
    ]
    f_halves = [f.astype(BF16) for f in f_halves]
    s_rows = move(low, lambda z, c: None if c else (z - 1, c))
    q_rows = jnp.concatenate(
        [jnp.where(first, q_half, other), jnp.where(first, other, q_half)], 1
    )
    pieces = share(True, s_rows, q_rows, f_halves)
    pieces = exchange(pieces).reshape(order, half + 2 * chunk)
    sigma = sigma + fold(pieces[:, half:], f_halves)
    low = sigma.astype(BF16)
    f_mine = after(pieces[:, :half], low)
    f_halves = (f_mine, from_second(f_mine))

    for done in range(planes - 2, 0, -2):
        s_rows = move(
            low,
            lambda z, c: (z - 2, c) if c == 0 and z in (done, done + 1) else None,
        )
        sigma = sigma + fold(turn(s_rows, f_halves), f_halves)
        low = sigma.astype(BF16)

    x_rows = move(low, lambda z, c: (z - 1, 1) if c == 0 else None)
    odd_halves = (odd_other, odd)
    update = fold(turn(x_rows, odd_halves), odd_halves)
    sigma = jnp.where(first, sigma, b_rows + update)

    low = sigma.astype(BF16)
    params = pltpu.CompilerParams(vmem_limit_bytes=20 * 2**20)
    cost = pl.CostEstimate(
        flops=2 * count * chunk * order * order,
        bytes_accessed=2 * count * order * order,
        transcendentals=0,
    )
    two = count // 2
    map_spec = pl.BlockSpec((two, order, order), lambda n: (n, 0, 0))
    sum_spec = pl.BlockSpec((two, chunk, order), lambda n: (n, 0, 0))
    v_rows = pl.pallas_call(
        interior_rows,
        grid=(2,),
        in_specs=[pl.BlockSpec((chunk, order), lambda n: (0, 0)), map_spec],
        out_specs=pl.BlockSpec((tiles, chunk, two * chunk), lambda n: (0, 0, n)),
        out_shape=jax.ShapeDtypeStruct((tiles, chunk, count * chunk), BF16),
        compiler_params=params,
        cost_estimate=cost,
    )(low, maps)
    v_cols = exchange(v_rows).reshape(order, count * chunk)
    interior_cov = pl.pallas_call(
        interior_sums,
        grid=(2,),
        in_specs=[
            pl.BlockSpec((order, two * chunk), lambda n: (0, n)),
            map_spec,
            sum_spec,
        ],
        out_specs=sum_spec,
        out_shape=jax.ShapeDtypeStruct((count, chunk, order), F32),
        compiler_params=params,
        cost_estimate=cost,
    )(v_cols, maps, interior_inv[0])
    return sigma[None], interior_cov[None]


def solution(mesh):
    in_specs = (
        P("tm", "tile", None),
        P("tm", "tile", None),
        P("tm", None, None, None),
        P("tm", None, "tile", None),
    )
    out_specs = (P("tm", "tile", None), P("tm", None, "tile", None))
    return jax.shard_map(shards, mesh=mesh, in_specs=in_specs, out_specs=out_specs, check_vma=False)
```

```python
import functools

import jax
import jax.numpy as jnp
from jax import lax
from jax.experimental import pallas as pl
from jax.experimental.pallas import tpu as pltpu
from jax.sharding import PartitionSpec as P

AXES = ("tm", "tile")
BF16 = jnp.bfloat16
F32 = jnp.float32


def dot(left, right, left_dim, right_dim):
    return lax.dot_general(
        left, right, (((left_dim,), (right_dim,)), ((), ())), preferred_element_type=F32
    )


def spread_rows(core_ref, own_ref, given_ref, out_ref):
    half = out_ref.shape[2]
    for core, ref in enumerate((own_ref, given_ref)):

        @pl.when(core_ref[0] == core)
        def _():
            rows = ref[:, core * half : (core + 1) * half]
            for t in range(out_ref.shape[0]):
                out_ref[t] = rows


def spread_products(with_rows, s_ref, rows_ref, mine_ref, other_ref, out_ref):
    tiles, rows, width = out_ref.shape
    lane = 2 * rows
    start = width - lane
    if with_rows is not None:
        all_rows = rows_ref[...]
        if with_rows:
            all_rows = jnp.dot(all_rows, mine_ref[...], preferred_element_type=F32)
            all_rows = all_rows.astype(BF16)
        for t in range(tiles):
            out_ref[t, :, :start] = all_rows
    t = 0
    for ref in (mine_ref, other_ref):
        product = jnp.dot(s_ref[...], ref[...], preferred_element_type=F32)
        for at in range(0, product.shape[1], lane):
            pair = product[:, at : at + lane]
            out_ref[t, :, start:] = pair.astype(BF16)
            out_ref[t + 1, :, start:] = pltpu.roll(pair, rows, 1).astype(BF16)
            t += 2


def interior_rows(sigma_ref, maps_ref, out_ref):
    sigma = sigma_ref[...].astype(BF16)
    count = maps_ref.shape[0]
    here, rows, width = out_ref.shape
    lane = 2 * width // count
    low = lax.broadcasted_iota(jnp.int32, (rows, lane), 1) < lane // 2
    for j in range(0, count, 2):
        one, two = [
            jnp.dot(sigma, maps_ref[j + i], preferred_element_type=F32) for i in range(2)
        ]
        to = pl.ds(j // 2 * lane, lane)
        for pair in range(here // 2):
            a = one[:, pair * lane : (pair + 1) * lane]
            b = two[:, pair * lane : (pair + 1) * lane]
            even = jnp.where(low, a, pltpu.roll(b, lane // 2, 1))
            odd = jnp.where(low, pltpu.roll(a, lane // 2, 1), b)
            out_ref[2 * pair, :, to] = even.astype(BF16)
            out_ref[2 * pair + 1, :, to] = odd.astype(BF16)


def interior_sums(cols_ref, maps_ref, inv_ref, out_ref):
    count, rows = inv_ref.shape[:2]
    turned = cols_ref[...].T
    for j in range(count):
        out_ref[j] = inv_ref[j] + jnp.dot(
            turned[j * rows : (j + 1) * rows], maps_ref[j], preferred_element_type=F32
        )


def shards(boundary_inv, coupling, interior_map, interior_inv):
    planes = lax.axis_size("tm") // 2
    tiles = lax.axis_size("tile")
    first = lax.axis_index("tm") % 2 == 0
    chunk, order = boundary_inv.shape[1:]
    half = order // 2

    def move(value, route):
        pairs = []
        for z in range(planes):
            for c in range(2):
                to = route(z, c)
                if to is not None and 0 <= to[0] < planes:
                    for t in range(tiles):
                        source, target = 2 * z + c, 2 * to[0] + to[1]
                        pairs.append((source * tiles + t, target * tiles + t))
        return lax.ppermute(value, AXES, pairs)

    def swap_cores(value):
        return move(value, lambda z, c: (z, 1 - c))

    def from_first(value):
        return move(value, lambda z, c: (z, 1) if c == 0 else None)

    def from_second(value):
        return move(value, lambda z, c: (z, 0) if c else None)

    def exchange(pieces):
        return lax.all_to_all(pieces, "tile", 0, 0)

    def placed(kernel, width):
        return pl.pallas_call(
            kernel,
            out_shape=pltpu.VMEM((tiles, chunk, width), BF16),
            compiler_params=pltpu.CompilerParams(vmem_limit_bytes=12 * 2**20),
        )

    def times(left, left_dim, halves):
        return jnp.concatenate([dot(left, h, left_dim, 0) for h in halves], 1)

    def fold(w_cols, halves):
        return times(w_cols, 0, halves)[:chunk]

    def turn(s_rows, f_halves):
        pieces = placed(functools.partial(spread_products, None), 2 * chunk)(
            s_rows, s_rows, *f_halves
        )
        return exchange(pieces).reshape(order, 2 * chunk)

    def share(with_rows, s_rows, rows, f_halves):
        pieces = placed(functools.partial(spread_products, with_rows), half + 2 * chunk)(
            s_rows, rows, *f_halves
        )
        return pieces

    b_rows = boundary_inv[0]
    f_rows = coupling[0]
    maps = interior_map[0]
    count = maps.shape[0]

    given = swap_cores(f_rows)
    q_rows = jnp.where(first, given, f_rows)
    odd = jnp.where(first, given[:, :half], f_rows[:, half:])
    s_rows = from_second(b_rows.astype(BF16))

    def after(value, anchor):
        return lax.optimization_barrier((value, anchor))[0]

    whole = pl.BlockSpec(memory_space=pltpu.VMEM)
    pieces = pl.pallas_call(
        spread_rows,
        in_specs=[pl.BlockSpec(memory_space=pltpu.SMEM), whole, whole],
        out_shape=pltpu.VMEM((tiles, chunk, half), BF16),
        compiler_params=pltpu.CompilerParams(vmem_limit_bytes=12 * 2**20),
    )((lax.axis_index("tm") % 2).astype(jnp.int32).reshape(1), f_rows, given)
    f_mine = exchange(pieces).reshape(order, half)
    f_halves = (f_mine, from_second(f_mine))

    q_half = dot(q_rows, f_mine, 1, 0).astype(BF16)
    q_half = move(q_half, lambda z, c: (z - 1, c))
    pieces = share(False, s_rows, odd, f_halves)
    other = swap_cores(q_half)
    pieces = exchange(pieces).reshape(order, half + 2 * chunk)
    odd = pieces[:, :half]
    odd_other = swap_cores(odd)
    sigma = b_rows + fold(pieces[:, half:], f_halves)
    low = sigma.astype(BF16)

    own = jnp.where(first, 0, half)
    f_halves = [
        dot(odd, lax.dynamic_slice_in_dim(f, own, half, 0), 1, 0)
        + dot(odd_other, lax.dynamic_slice_in_dim(f, half - own, half, 0), 1, 0)
        for f in after(f_halves, low)
    ]
    f_halves = [f.astype(BF16) for f in f_halves]
    s_rows = move(low, lambda z, c: None if c else (z - 1, c))
    q_rows = jnp.concatenate(
        [jnp.where(first, q_half, other), jnp.where(first, other, q_half)], 1
    )
    pieces = share(True, s_rows, q_rows, f_halves)
    pieces = exchange(pieces).reshape(order, half + 2 * chunk)
    sigma = sigma + fold(pieces[:, half:], f_halves)
    low = sigma.astype(BF16)
    f_mine = after(pieces[:, :half], low)
    f_halves = (f_mine, from_second(f_mine))

    for done in range(planes - 2, 0, -2):
        s_rows = move(
            low,
            lambda z, c: (z - 2, c) if c == 0 and z in (done, done + 1) else None,
        )
        sigma = sigma + fold(turn(s_rows, f_halves), f_halves)
        low = sigma.astype(BF16)

    x_rows = move(low, lambda z, c: (z - 1, 1) if c == 0 else None)
    odd_halves = (odd_other, odd)
    update = fold(turn(x_rows, odd_halves), odd_halves)
    sigma = jnp.where(first, sigma, b_rows + update)

    params = pltpu.CompilerParams(vmem_limit_bytes=20 * 2**20)
    cost = pl.CostEstimate(
        flops=2 * count * chunk * order * order,
        bytes_accessed=2 * count * order * order,
        transcendentals=0,
    )
    two = count // 2
    map_spec = pl.BlockSpec((two, order, order), lambda n: (n, 0, 0))
    sum_spec = pl.BlockSpec((two, chunk, order), lambda n: (n, 0, 0))
    v_rows = pl.pallas_call(
        interior_rows,
        grid=(2,),
        in_specs=[pl.BlockSpec((chunk, order), lambda n: (0, 0)), map_spec],
        out_specs=pl.BlockSpec((tiles, chunk, two * chunk), lambda n: (0, 0, n)),
        out_shape=jax.ShapeDtypeStruct((tiles, chunk, count * chunk), BF16),
        compiler_params=params,
        cost_estimate=cost,
    )(sigma, maps)
    v_cols = exchange(v_rows).reshape(order, count * chunk)
    interior_cov = pl.pallas_call(
        interior_sums,
        grid=(2,),
        in_specs=[
            pl.BlockSpec((order, two * chunk), lambda n: (0, n)),
            map_spec,
            sum_spec,
        ],
        out_specs=sum_spec,
        out_shape=jax.ShapeDtypeStruct((count, chunk, order), F32),
        compiler_params=params,
        cost_estimate=cost,
    )(v_cols, maps, interior_inv[0])
    return sigma[None], interior_cov[None]


def solution(mesh):
    in_specs = (
        P("tm", "tile", None),
        P("tm", "tile", None),
        P("tm", None, None, None),
        P("tm", None, "tile", None),
    )
    out_specs = (P("tm", "tile", None), P("tm", None, "tile", None))
    return jax.shard_map(shards, mesh=mesh, in_specs=in_specs, out_specs=out_specs, check_vma=False)
```

```python
import functools

import jax
import jax.numpy as jnp
from jax import lax
from jax.experimental import pallas as pl
from jax.experimental.pallas import tpu as pltpu
from jax.sharding import PartitionSpec as P

AXES = ("tm", "tile")
BF16 = jnp.bfloat16
F32 = jnp.float32


def dot(left, right, left_dim, right_dim):
    return lax.dot_general(
        left, right, (((left_dim,), (right_dim,)), ((), ())), preferred_element_type=F32
    )


def spread_rows(rows_ref, out_ref):
    for t in range(out_ref.shape[0]):
        out_ref[t] = rows_ref[...]


def spread_products(with_rows, s_ref, rows_ref, mine_ref, other_ref, out_ref):
    tiles, rows, width = out_ref.shape
    lane = 2 * rows
    start = width - lane
    if with_rows is not None:
        all_rows = rows_ref[...]
        if with_rows:
            all_rows = jnp.dot(all_rows, mine_ref[...], preferred_element_type=F32)
            all_rows = all_rows.astype(BF16)
        for t in range(tiles):
            out_ref[t, :, :start] = all_rows
    t = 0
    for ref in (mine_ref, other_ref):
        product = jnp.dot(s_ref[...], ref[...], preferred_element_type=F32)
        for at in range(0, product.shape[1], lane):
            pair = product[:, at : at + lane]
            out_ref[t, :, start:] = pair.astype(BF16)
            out_ref[t + 1, :, start:] = pltpu.roll(pair, rows, 1).astype(BF16)
            t += 2


def interior_rows(sigma_ref, maps_ref, out_ref):
    sigma = sigma_ref[...].astype(BF16)
    count = maps_ref.shape[0]
    here, rows, width = out_ref.shape
    lane = 2 * width // count
    low = lax.broadcasted_iota(jnp.int32, (rows, lane), 1) < lane // 2
    for j in range(0, count, 2):
        one, two = [
            jnp.dot(sigma, maps_ref[j + i], preferred_element_type=F32) for i in range(2)
        ]
        to = pl.ds(j // 2 * lane, lane)
        for pair in range(here // 2):
            a = one[:, pair * lane : (pair + 1) * lane]
            b = two[:, pair * lane : (pair + 1) * lane]
            even = jnp.where(low, a, pltpu.roll(b, lane // 2, 1))
            odd = jnp.where(low, pltpu.roll(a, lane // 2, 1), b)
            out_ref[2 * pair, :, to] = even.astype(BF16)
            out_ref[2 * pair + 1, :, to] = odd.astype(BF16)


def interior_sums(cols_ref, maps_ref, inv_ref, out_ref):
    count, rows = inv_ref.shape[:2]
    turned = cols_ref[...].T
    for j in range(count):
        out_ref[j] = inv_ref[j] + jnp.dot(
            turned[j * rows : (j + 1) * rows], maps_ref[j], preferred_element_type=F32
        )


def shards(boundary_inv, coupling, interior_map, interior_inv):
    planes = lax.axis_size("tm") // 2
    tiles = lax.axis_size("tile")
    first = lax.axis_index("tm") % 2 == 0
    chunk, order = boundary_inv.shape[1:]
    half = order // 2

    def move(value, route):
        pairs = []
        for z in range(planes):
            for c in range(2):
                to = route(z, c)
                if to is not None and 0 <= to[0] < planes:
                    for t in range(tiles):
                        source, target = 2 * z + c, 2 * to[0] + to[1]
                        pairs.append((source * tiles + t, target * tiles + t))
        return lax.ppermute(value, AXES, pairs)

    def swap_cores(value):
        return move(value, lambda z, c: (z, 1 - c))

    def from_first(value):
        return move(value, lambda z, c: (z, 1) if c == 0 else None)

    def from_second(value):
        return move(value, lambda z, c: (z, 0) if c else None)

    def exchange(pieces):
        return lax.all_to_all(pieces, "tile", 0, 0)

    def gather(value):
        return exchange(placed(spread_rows, value.shape[1])(value))

    def placed(kernel, width):
        return pl.pallas_call(
            kernel,
            out_shape=pltpu.VMEM((tiles, chunk, width), BF16),
            compiler_params=pltpu.CompilerParams(vmem_limit_bytes=12 * 2**20),
        )

    def times(left, left_dim, halves):
        return jnp.concatenate([dot(left, h, left_dim, 0) for h in halves], 1)

    def fold(w_cols, halves):
        return times(w_cols, 0, halves)[:chunk]

    def turn(s_rows, f_halves):
        pieces = placed(functools.partial(spread_products, None), 2 * chunk)(
            s_rows, s_rows, *f_halves
        )
        return exchange(pieces).reshape(order, 2 * chunk)

    def share(with_rows, s_rows, rows, f_halves):
        pieces = placed(functools.partial(spread_products, with_rows), half + 2 * chunk)(
            s_rows, rows, *f_halves
        )
        return pieces

    b_rows = boundary_inv[0]
    f_rows = coupling[0]
    maps = interior_map[0]
    count = maps.shape[0]

    given = swap_cores(f_rows)
    q_rows = jnp.where(first, given, f_rows)
    f_half = jnp.where(first, f_rows[:, :half], given[:, half:])
    odd = jnp.where(first, given[:, :half], f_rows[:, half:])
    s_rows = from_second(b_rows.astype(BF16))

    def after(value, anchor):
        return lax.optimization_barrier((value, anchor))[0]

    f_mine = gather(f_half).reshape(order, half)
    f_halves = (f_mine, from_second(f_mine))

    q_half = dot(q_rows, f_mine, 1, 0).astype(BF16)
    q_half = move(q_half, lambda z, c: (z - 1, c))
    pieces = share(False, s_rows, odd, f_halves)
    other = swap_cores(q_half)
    pieces = exchange(pieces).reshape(order, half + 2 * chunk)
    odd = pieces[:, :half]
    odd_other = swap_cores(odd)
    sigma = b_rows + fold(pieces[:, half:], f_halves)
    low = sigma.astype(BF16)

    own = jnp.where(first, 0, half)
    f_halves = [
        dot(odd, lax.dynamic_slice_in_dim(f, own, half, 0), 1, 0)
        + dot(odd_other, lax.dynamic_slice_in_dim(f, half - own, half, 0), 1, 0)
        for f in after(f_halves, low)
    ]
    f_halves = [f.astype(BF16) for f in f_halves]
    s_rows = move(low, lambda z, c: None if c else (z - 1, c))
    q_rows = jnp.concatenate(
        [jnp.where(first, q_half, other), jnp.where(first, other, q_half)], 1
    )
    pieces = share(True, s_rows, q_rows, f_halves)
    pieces = exchange(pieces).reshape(order, half + 2 * chunk)
    sigma = sigma + fold(pieces[:, half:], f_halves)
    low = sigma.astype(BF16)
    f_mine = after(pieces[:, :half], low)
    f_halves = (f_mine, from_second(f_mine))

    for done in range(planes - 2, 0, -2):
        s_rows = move(
            low,
            lambda z, c: (z - 2, c) if c == 0 and z in (done, done + 1) else None,
        )
        sigma = sigma + fold(turn(s_rows, f_halves), f_halves)
        low = sigma.astype(BF16)

    x_rows = move(low, lambda z, c: (z - 1, 1) if c == 0 else None)
    odd_halves = (odd_other, odd)
    update = fold(turn(x_rows, odd_halves), odd_halves)
    sigma = jnp.where(first, sigma, b_rows + update)

    params = pltpu.CompilerParams(vmem_limit_bytes=20 * 2**20)
    cost = pl.CostEstimate(
        flops=2 * count * chunk * order * order,
        bytes_accessed=2 * count * order * order,
        transcendentals=0,
    )
    two = count // 2
    map_spec = pl.BlockSpec((two, order, order), lambda n: (n, 0, 0))
    sum_spec = pl.BlockSpec((two, chunk, order), lambda n: (n, 0, 0))
    v_rows = pl.pallas_call(
        interior_rows,
        grid=(2,),
        in_specs=[pl.BlockSpec((chunk, order), lambda n: (0, 0)), map_spec],
        out_specs=pl.BlockSpec((tiles, chunk, two * chunk), lambda n: (0, 0, n)),
        out_shape=jax.ShapeDtypeStruct((tiles, chunk, count * chunk), BF16),
        compiler_params=params,
        cost_estimate=cost,
    )(sigma, maps)
    v_cols = exchange(v_rows).reshape(order, count * chunk)
    interior_cov = pl.pallas_call(
        interior_sums,
        grid=(2,),
        in_specs=[
            pl.BlockSpec((order, two * chunk), lambda n: (0, n)),
            map_spec,
            sum_spec,
        ],
        out_specs=sum_spec,
        out_shape=jax.ShapeDtypeStruct((count, chunk, order), F32),
        compiler_params=params,
        cost_estimate=cost,
    )(v_cols, maps, interior_inv[0])
    return sigma[None], interior_cov[None]


def solution(mesh):
    in_specs = (
        P("tm", "tile", None),
        P("tm", "tile", None),
        P("tm", None, None, None),
        P("tm", None, "tile", None),
    )
    out_specs = (P("tm", "tile", None), P("tm", None, "tile", None))
    return jax.shard_map(shards, mesh=mesh, in_specs=in_specs, out_specs=out_specs, check_vma=False)
```
